256 devices in a mesh: sec: 2 (over z_hi), gx: 32 (over y, x, core), gz: 4 (over z_lo).
Axes of the slice: x: 4, y: 4, z: 8 (z_hi: 2, z_lo: 4; z = z_hi * 4 + z_lo), core: 2. Of those that a mesh axis runs over, the one named last changes fastest.
Arguments:
- velocity: float32 [2, 3, 1024, 32, 512], P('sec', None, 'gx', 'gz'), may hold values from -6 to 6
- drag: float32 [2, 1024, 32, 512], P('sec', 'gx', 'gz'), may hold values from 0.2 to 2
- stream_gain: float32 [513], replicated, may hold values from 0.5 to 2
- span_gain: float32 [257], replicated, may hold values from 0.5 to 2
Outputs:
- advanced: float32 [2, 3, 1024, 32, 512], P('sec', None, 'gx', 'gz')
The draws below stay inside these ranges and needn't reach their ends.
All inputs are finite; a program needn't handle non-finite values.
Results may differ from the reference program's by a relative error of at most 0.00005.
Values sent between devices are 32-bit elements; how exact they have to be, the bound alone decides.
A program may use at most 128 MiB of HBM per device.

```python
import math
import jax
import jax.numpy as jnp

NY = 512
NX = 1024
NZ = 32


def shard_levels(key, shape, pieces, least, largest):
    factor_of, own = 1.0, jax.random.fold_in(key, 6)
    for axis_at, shards_of in pieces:
        steps = jnp.exp(jax.random.uniform(jax.random.fold_in(own, axis_at), (shards_of,), jnp.float32, least / len(pieces), largest / len(pieces)))
        factor_of = factor_of * jnp.repeat(steps, shape[axis_at] // shards_of).reshape([-1 if axis == axis_at else 1 for axis in range(len(shape))])
    return factor_of


def gaussian(stream_key, shape, spread, most, shards=(), kind=jnp.bfloat16):
    values = jax.random.normal(stream_key, shape, jnp.float32) * spread
    if len(shards) > 0:
        values = shard_levels(stream_key, shape, shards, -0.22, 0.18) * values
    return jnp.clip(values, min=-most, max=most).astype(kind)


def setup_inputs(seed: int = 0) -> dict:
    streams_of = jax.random.split(jax.random.key(seed), 5)
    velocity = gaussian(streams_of[0], (2, 3, NX, NZ, NY), 1.0, 6.0, ((0, 2), (2, 32), (3, 4)), jnp.float32)
    drag = jnp.clip(jnp.exp(math.log(2.0) - 2.3025851 * jax.random.uniform(streams_of[1], (2, NX, NZ, NY), jnp.float32) ** shard_levels(streams_of[1], (2, NX, NZ, NY), ((0, 2), (1, 32), (2, 4)), -0.2, 0.2)), 0.2, 2.0)
    stream_gain = jnp.clip(jnp.exp(jax.random.uniform(streams_of[2], (NX // 2 + 1,), jnp.float32, math.log(0.5), math.log(2.0))), 0.5, 2.0)
    span_gain = jnp.clip(jnp.exp(jax.random.uniform(streams_of[3], (NY // 2 + 1,), jnp.float32, math.log(0.5), math.log(2.0))), 0.5, 2.0)
    return dict(velocity=velocity, drag=drag, stream_gain=stream_gain, span_gain=span_gain)


fringe_peak = 4.0
time_step = 0.05


def spectral(signal, along, gains):
    length = signal.shape[along]
    modes = jnp.arange(length // 2 + 1)
    wavenum = jnp.where(modes == length // 2, 0.0, 2.0 * jnp.pi * modes / length) * gains
    dims_shape = [1] * signal.ndim
    dims_shape[along] = length // 2 + 1
    spectrum = jnp.fft.rfft(signal, axis=along)
    result = jnp.fft.irfft(1j * wavenum.reshape(dims_shape) * spectrum, n=length, axis=along)
    return result.astype(signal.dtype)


def tendency(fields, drag, stream_gain, span_gain):
    grad_x = spectral(fields, 2, stream_gain)
    grad_y = spectral(fields, 4, span_gain)
    padded = jnp.pad(fields, ((0, 0), (0, 0), (0, 0), (1, 1), (0, 0)))
    grad_z = 0.5 * (padded[:, :, :, 2:] - padded[:, :, :, :-2])
    advect = fields[:, 0:1] * grad_x + fields[:, 1:2] * grad_y + fields[:, 2:3] * grad_z
    cells = jnp.arange(NX)
    fringe_start = 3 * NX // 4
    fringe_width = NX // 4
    phases = (cells - fringe_start).astype(jnp.float32) + 0.5
    profile = jnp.where(cells >= fringe_start, fringe_peak * jnp.sin(jnp.pi * phases / fringe_width) ** 2, 0.0)
    relax = profile[None, :, None, None] * (fields[0] - fields[1])
    forcing = jnp.stack([jnp.zeros_like(relax), relax])
    resist = -drag[:, None] * jnp.abs(fields[:, 0:1]) * fields
    return -advect + resist + forcing


def reference(velocity, drag, stream_gain, span_gain):
    first = velocity + time_step * tendency(velocity, drag, stream_gain, span_gain)
    return 0.5 * velocity + 0.5 * (first + time_step * tendency(first, drag, stream_gain, span_gain))
```

```python
import functools

import jax
import jax.numpy as jnp
import ml_dtypes
import numpy as np
from jax import lax
from jax.experimental import pallas as pl
from jax.experimental.pallas import tpu as pltpu
from jax.sharding import PartitionSpec as P

MESH = pl.DeviceIdType.MESH
ANY = pl.ANY
F32 = jnp.float32
BF16 = jnp.bfloat16
fringe_peak = 4.0
dt = 0.05
LANES = 128


def halves(x):
    high = x.astype(np.float32).astype(ml_dtypes.bfloat16)
    low = (x - high.astype(np.float64)).astype(ml_dtypes.bfloat16)
    return high, low


def transform_tables(half):
    points = np.arange(half, dtype=np.int64)
    forward, inverse = [], []
    for odd in range(2):
        modes = 2 * np.arange(half // 2, dtype=np.int64) + odd
        angle = 2.0 * np.pi * (np.outer(modes, points) % (2 * half)) / (2 * half)
        forward.append(np.concatenate([np.cos(angle), np.sin(angle)], 0))
        inverse.append(np.concatenate([-np.sin(angle), np.cos(angle)], 0).T)
    return np.stack(forward), np.stack(inverse)


def mode_weights(stream_gain, span_gain, total_x, width_y):
    wave_y = (-(2.0 / width_y) * 2.0 * np.pi / width_y) * np.arange(width_y // 2)
    wave_x = ((2.0 / total_x) * 2.0 * np.pi / total_x) * np.arange(total_x // 2)
    along_y = span_gain[: width_y // 2] * wave_y.astype(np.float32)
    along_x = (stream_gain[: total_x // 2] * wave_x.astype(np.float32)).reshape(-1, 2)
    rows = jnp.stack([along_y, along_x[:, 0], along_x[:, 1]])
    return jnp.concatenate([rows, rows], 1)


def split(x):
    high = x.astype(BF16)
    return high, (x - high.astype(F32)).astype(BF16)


def dot(a, b):
    return jnp.dot(a, b, preferred_element_type=F32)


def step_kernel(
    groups, sheets, v_hbm, drag_hbm, weights, forward_hbm, inverse_hbm, lam_hbm, out_hbm,
    v_raw, drag_raw, out_raw, forward, inverse, lam, table,
    v_here, f_here, drag, h_here, g_here, partial, stack, span_grad,
    v_pen, h_pen, f_pen, g_pen, rest, up_v, up_f,
    load_sem, own_sem, send_sem, recv_sem, halo_send, halo_recv, up_send, up_recv,
):
    me, gz, sec = lax.axis_index("gx"), lax.axis_index("gz"), lax.axis_index("sec")
    levels, cells, width = drag.shape
    half = table.shape[-1]
    total = 2 * half
    bands = width // LANES
    fringe = total - total // 4
    shape_y, shape_x = 4, groups // 8

    def peer(k):
        y, x, core = me // (2 * shape_x), (me // 2) % shape_x, me % 2
        y = (y + k // (2 * shape_x)) % shape_y
        x = (x + (k // 2) % shape_x) % shape_x
        return (y * shape_x + x) * 2 + (core + k) % 2

    def rows_of(device):
        return pl.ds(pl.multiple_of(device * cells, cells), cells)

    def band_of(device):
        return pl.ds(pl.multiple_of((device % bands) * LANES, LANES), LANES)

    def wait(ref, sem):
        pltpu.make_async_copy(ref, ref, sem).wait()

    def remote(source, target, sent, arrived, where):
        pltpu.make_async_remote_copy(
            source, target, sent, arrived, device_id=where, device_id_type=MESH
        ).start()

    def to_pencils(source, base, target, comps, slot):
        def block(p):
            return source.at[comps, base + p // bands, :, band_of(p)]

        def body(k, carry):
            p = peer(k)
            remote(block(p), target.at[comps, rows_of(me)], send_sem.at[slot], recv_sem.at[slot], {"gx": p})
            return carry

        lax.fori_loop(1, groups, body, 0)
        pltpu.make_async_copy(block(me), target.at[comps, rows_of(me)], recv_sem.at[slot]).start()

    def to_blocks(source, target, base, comp, slot):
        place = target.at[comp, base + me // bands, :, band_of(me)]

        def body(k, carry):
            p = peer(k)
            remote(source.at[comp, rows_of(p)], place, send_sem.at[slot], recv_sem.at[slot], {"gx": p})
            return carry

        lax.fori_loop(1, groups, body, 0)
        pltpu.make_async_copy(source.at[comp, rows_of(me)], place, recv_sem.at[slot]).start()

    def send_halo(fields, slot):
        @pl.when(gz > 0)
        def _():
            remote(fields.at[:, 1], fields.at[:, levels + 1], halo_send.at[slot, 0], halo_recv.at[slot, 0], {"gz": gz - 1})

        @pl.when(gz < sheets - 1)
        def _():
            remote(fields.at[:, levels], fields.at[:, 0], halo_send.at[slot, 1], halo_recv.at[slot, 1], {"gz": gz + 1})

    def wait_halo(fields, slot):
        @pl.when(gz > 0)
        def _():
            wait(fields.at[:, 0], halo_recv.at[slot, 1])

        @pl.when(gz < sheets - 1)
        def _():
            wait(fields.at[:, levels + 1], halo_recv.at[slot, 0])

    def wait_halo_sent(fields, slot):
        @pl.when(gz > 0)
        def _():
            wait(fields.at[:, 1], halo_send.at[slot, 0])

        @pl.when(gz < sheets - 1)
        def _():
            wait(fields.at[:, levels], halo_send.at[slot, 1])

    loads = [pltpu.make_async_copy(v_hbm.at[c], v_raw.at[c], load_sem.at[c]) for c in range(3)]
    loads += [
        pltpu.make_async_copy(inverse_hbm, inverse, load_sem.at[3]),
        pltpu.make_async_copy(forward_hbm, forward, load_sem.at[4]),
        pltpu.make_async_copy(drag_hbm, drag_raw, load_sem.at[5]),
        pltpu.make_async_copy(lam_hbm, lam, load_sem.at[6]),
    ]
    for load in loads:
        load.start()
    barrier = pltpu.get_barrier_semaphore()

    def greet(k, carry):
        pl.semaphore_signal(barrier, inc=1, device_id={"gx": peer(k)}, device_id_type=MESH)
        return carry

    lax.fori_loop(1, groups, greet, 0)
    pl.semaphore_signal(barrier, inc=1, device_id={"sec": 1 - sec}, device_id_type=MESH)

    @pl.when(gz > 0)
    def _():
        pl.semaphore_signal(barrier, inc=1, device_id={"gz": gz - 1}, device_id_type=MESH)

    @pl.when(gz < sheets - 1)
    def _():
        pl.semaphore_signal(barrier, inc=1, device_id={"gz": gz + 1}, device_id_type=MESH)

    for c in range(3):
        loads[c].wait()
        for z in range(levels):
            v_here[c, 1 + z] = v_raw[c, :, z, :]

    @pl.when((gz == 0) | (gz == sheets - 1))
    def _():
        pl.semaphore_wait(barrier, groups + 1)

    @pl.when((gz > 0) & (gz < sheets - 1))
    def _():
        pl.semaphore_wait(barrier, groups + 2)

    send_halo(v_here, 0)
    to_pencils(v_here, 1, v_pen, slice(None), 0)

    @pl.when(gz == 0)
    def _():
        v_here[:, 0] = jnp.zeros((3, cells, width), F32)
        f_here[:, 0] = jnp.zeros((3, cells, width), F32)

    @pl.when(gz == sheets - 1)
    def _():
        v_here[:, levels + 1] = jnp.zeros((3, cells, width), F32)
        f_here[:, levels + 1] = jnp.zeros((3, cells, width), F32)

    loads[3].wait()
    loads[4].wait()

    def build(j, carry):
        kind = j // 2
        scaled_high, scaled_low = split(inverse[kind] * weights[pl.ds(j, 1), :])
        matrix = dot(scaled_high, forward[kind, 0]) + (
            dot(scaled_low, forward[kind, 0]) + dot(scaled_high, forward[kind, 1])
        )
        table[j, 0], table[j, 1] = split(matrix)
        return carry

    lax.fori_loop(0, 3, build, 0)
    loads[5].wait()
    for z in range(levels):
        drag[z] = drag_raw[:, z, :]

    def local_terms(fields, comp, put):
        def spread(z, carry):
            at = pl.ds(pl.multiple_of(z * cells, cells), cells)
            low_at = pl.ds(pl.multiple_of((levels + z) * cells, cells), cells)
            stack[at], stack[low_at] = split(fields[comp, 1 + z])
            return carry

        lax.fori_loop(0, levels, spread, 0)
        rows = levels * cells
        both = dot(stack[...], table[0, 0])
        span_grad[...] = (both[:rows] + both[rows:]) + dot(stack[:rows], table[0, 1])

        def level(z, carry):
            at = pl.ds(pl.multiple_of(z * cells, cells), cells)
            rise = 0.5 * (fields[comp, 2 + z] - fields[comp, z])
            here = fields[comp, 1 + z]
            advect = fields[1, 1 + z] * span_grad[at] + fields[2, 1 + z] * rise
            put(z, here, -advect - drag[z] * jnp.abs(fields[0, 1 + z]) * here)
            return carry

        lax.fori_loop(0, levels, level, 0)

    def stream_grad(fields, comp):
        near, far = fields[comp, :half], fields[comp, half:]
        parts = []
        for j, mixed in ((1, near + far), (2, near - far)):
            high, low = split(mixed)
            both = dot(table[j, 0], jnp.concatenate([high, low], 1))
            parts.append((both[:, :LANES] + both[:, LANES:]) + dot(table[j, 1], high))
        return parts[0] + parts[1], parts[0] - parts[1]

    wait_halo(v_here, 0)
    for c in range(3):

        def keep(z, here, value, c=c):
            h_here[c, z] = value

        local_terms(v_here, c, keep)
        to_pencils(h_here, 0, h_pen, c, 1 + c)

    loads[6].wait()
    wait(v_pen, recv_sem.at[0])
    lift = pl.ds(fringe, total - fringe)

    @pl.when(sec == 0)
    def _():
        remote(v_pen.at[:, lift], up_v, up_send.at[0], up_recv.at[0], {"sec": 1})

    for c in range(3):
        near, far = stream_grad(v_pen, c)
        rest[c, :half] = v_pen[c, :half] - dt * (v_pen[0, :half] * near)
        rest[c, half:] = v_pen[c, half:] - dt * (v_pen[0, half:] * far)

    @pl.when(sec == 1)
    def _():
        wait(up_v, up_recv.at[0])
        for c in range(3):
            rest[c, lift] += dt * (lam[...] * (up_v[c] - v_pen[c, lift]))

    for c in range(3):
        wait(h_pen.at[c], recv_sem.at[1 + c])
        f_pen[c] = rest[c] + dt * h_pen[c]
        to_blocks(f_pen, f_here, 1, c, 4 + c)

        @pl.when(sec == 0)
        def _(c=c):
            remote(f_pen.at[c, lift], up_f.at[c], up_send.at[1 + c], up_recv.at[1 + c], {"sec": 1})

    for c in range(3):
        near, far = stream_grad(f_pen, c)
        g_pen[c, :half] = -f_pen[0, :half] * near
        g_pen[c, half:] = -f_pen[0, half:] * far

        @pl.when(sec == 1)
        def _(c=c):
            wait(up_f.at[c], up_recv.at[1 + c])
            g_pen[c, lift] += lam[...] * (up_f[c] - f_pen[c, lift])

        to_blocks(g_pen, g_here, 0, c, 7 + c)

    for c in range(3):
        wait(g_here.at[c], recv_sem.at[4 + c])
    send_halo(f_here, 1)
    wait_halo(f_here, 1)
    for c in range(3):

        def keep(z, here, value, c=c):
            partial[c, z] = 0.5 * v_here[c, 1 + z] + 0.5 * (here + dt * value)

        local_terms(f_here, c, keep)

    stores = []
    for c in range(3):
        wait(g_here.at[c], recv_sem.at[7 + c])
        for z in range(levels):
            out_raw[c, :, z, :] = partial[c, z] + (0.5 * dt) * g_here[c, z]
        store = pltpu.make_async_copy(out_raw.at[c], out_hbm.at[c], own_sem.at[c])
        store.start()
        stores.append(store)

    others = pl.ds(0, total - cells)
    wait(v_pen.at[:, others], send_sem.at[0])
    for slot in range(1, 10):
        wait(v_pen.at[0, others], send_sem.at[slot])
    wait_halo_sent(v_here, 0)
    wait_halo_sent(f_here, 1)

    @pl.when(sec == 0)
    def _():
        wait(up_v, up_send.at[0])
        for c in range(3):
            wait(up_f.at[c], up_send.at[1 + c])

    for store in stores:
        store.wait()


def solution(mesh):
    groups, sheets = mesh.shape["gx"], mesh.shape["gz"]

    def shards(velocity, drag, stream_gain, span_gain):
        fields, drag_here = velocity[0], drag[0]
        _, cells, levels, width = fields.shape
        total = cells * groups
        half = total // 2
        pencil = (3, total, LANES)
        block = (3, levels, cells, width)
        padded = (3, levels + 2, cells, width)
        fringe = total // 4
        forward, inverse = transform_tables(half)
        high, low = halves(forward)
        forward = np.stack([high, low], 1)
        phases = np.pi * (np.arange(fringe) + 0.5) / fringe
        lam = np.repeat((fringe_peak * np.sin(phases) ** 2)[:, None], LANES, 1)
        weights = mode_weights(stream_gain, span_gain, total, width)
        dma = pltpu.SemaphoreType.DMA
        flops = 2 * 3 * (2 * total * half * LANES * 4 + 2 * half * half * half * 3)
        out = pl.pallas_call(
            functools.partial(step_kernel, groups, sheets),
            name="fringe_step",
            out_shape=jax.ShapeDtypeStruct(fields.shape, F32),
            in_specs=[pl.BlockSpec(memory_space=ANY)] * 2
            + [pl.BlockSpec(memory_space=pltpu.VMEM)]
            + [pl.BlockSpec(memory_space=ANY)] * 3,
            out_specs=pl.BlockSpec(memory_space=ANY),
            scratch_shapes=[
                pltpu.VMEM(fields.shape, F32),
                pltpu.VMEM(drag_here.shape, F32),
                pltpu.VMEM(fields.shape, F32),
                pltpu.VMEM((2, 2, half, half), BF16),
                pltpu.VMEM((2, half, half), F32),
                pltpu.VMEM((fringe, LANES), F32),
                pltpu.VMEM((3, 2, half, half), BF16),
                pltpu.VMEM(padded, F32),
                pltpu.VMEM(padded, F32),
                pltpu.VMEM((levels, cells, width), F32),
                pltpu.VMEM(block, F32),
                pltpu.VMEM(block, F32),
                pltpu.VMEM(block, F32),
                pltpu.VMEM((2 * levels * cells, width), BF16),
                pltpu.VMEM((levels * cells, width), F32),
                pltpu.VMEM(pencil, F32),
                pltpu.VMEM(pencil, F32),
                pltpu.VMEM(pencil, F32),
                pltpu.VMEM(pencil, F32),
                pltpu.VMEM(pencil, F32),
                pltpu.VMEM((3, fringe, LANES), F32),
                pltpu.VMEM((3, fringe, LANES), F32),
                dma((7,)),
                dma((3,)),
                dma((10,)),
                dma((10,)),
                dma((2, 2)),
                dma((2, 2)),
                dma((4,)),
                dma((4,)),
            ],
            compiler_params=pltpu.CompilerParams(
                collective_id=0, has_side_effects=True, vmem_limit_bytes=56 * 2**20
            ),
            cost_estimate=pl.CostEstimate(flops=flops, bytes_accessed=10**7, transcendentals=0),
        )(fields, drag_here, weights, forward, inverse.astype(np.float32), lam.astype(np.float32))
        return out[None]

    return jax.shard_map(
        shards,
        mesh=mesh,
        in_specs=(P("sec", None, "gx", "gz", None), P("sec", "gx", "gz", None), P(), P()),
        out_specs=P("sec", None, "gx", "gz", None),
        check_vma=False,
    )
```

```python
import functools

import jax
import jax.numpy as jnp
import ml_dtypes
import numpy as np
from jax import lax
from jax.experimental import pallas as pl
from jax.experimental.pallas import tpu as pltpu
from jax.sharding import PartitionSpec as P

MESH = pl.DeviceIdType.MESH
ANY = pl.ANY
F32 = jnp.float32
BF16 = jnp.bfloat16
fringe_peak = 4.0
dt = 0.05
LANES = 128


def halves(x):
    high = x.astype(np.float32).astype(ml_dtypes.bfloat16)
    low = (x - high.astype(np.float64)).astype(ml_dtypes.bfloat16)
    return high, low


def transform_tables(half):
    points = np.arange(half, dtype=np.int64)
    forward, inverse = [], []
    for odd in range(2):
        modes = 2 * np.arange(half // 2, dtype=np.int64) + odd
        angle = 2.0 * np.pi * (np.outer(modes, points) % (2 * half)) / (2 * half)
        forward.append(np.concatenate([np.cos(angle), np.sin(angle)], 0))
        inverse.append(np.concatenate([-np.sin(angle), np.cos(angle)], 0).T)
    return np.stack(forward), np.stack(inverse)


def mode_weights(stream_gain, span_gain, total_x, width_y):
    wave_y = (-(2.0 / width_y) * 2.0 * np.pi / width_y) * np.arange(width_y // 2)
    wave_x = ((2.0 / total_x) * 2.0 * np.pi / total_x) * np.arange(total_x // 2)
    along_y = span_gain[: width_y // 2] * wave_y.astype(np.float32)
    along_x = (stream_gain[: total_x // 2] * wave_x.astype(np.float32)).reshape(-1, 2)
    rows = jnp.stack([along_y, along_x[:, 0], along_x[:, 1]])
    return jnp.concatenate([rows, rows], 1)


def split(x):
    high = x.astype(BF16)
    return high, (x - high.astype(F32)).astype(BF16)


def dot(a, b):
    return jnp.dot(a, b, preferred_element_type=F32)


def step_kernel(
    groups, sheets, v_hbm, drag_hbm, weights, forward_hbm, inverse_hbm, lam_hbm, out_hbm,
    v_raw, drag_raw, out_raw, forward, inverse, lam, table,
    v_here, f_here, drag, h_here, g_here, partial, stack, span_grad,
    v_pen, h_pen, f_pen, g_pen, rest, up_v, up_f,
    load_sem, own_sem, send_sem, recv_sem, halo_send, halo_recv, up_send, up_recv,
):
    me, gz, sec = lax.axis_index("gx"), lax.axis_index("gz"), lax.axis_index("sec")
    levels, cells, width = drag.shape
    half = table.shape[-1]
    total = 2 * half
    bands = width // LANES
    fringe = total - total // 4
    lift = pl.ds(fringe, total - fringe)
    shape_y, shape_x = 4, groups // 8

    far_first = sorted(
        [(y, x, core) for y in range(shape_y) for x in range(shape_x) for core in range(2)][1:],
        key=lambda o: -(min(o[0], shape_y - o[0]) + min(o[1], shape_x - o[1])),
    )

    def peer(offset):
        y = (me // (2 * shape_x) + offset[0]) % shape_y
        x = (me // 2 + offset[1]) % shape_x
        return (y * shape_x + x) * 2 + (me + offset[2]) % 2

    def rows_of(device):
        return pl.ds(pl.multiple_of(device * cells, cells), cells)

    def band_of(device):
        return pl.ds(pl.multiple_of((device % bands) * LANES, LANES), LANES)

    def wait(ref, sem):
        pltpu.make_async_copy(ref, ref, sem).wait()

    def remote(source, target, sent, arrived, where):
        pltpu.make_async_remote_copy(
            source, target, sent, arrived, device_id=where, device_id_type=MESH
        ).start()

    def to_pencils(source, base, target, comp, slot):
        def block(p):
            return source.at[comp, base + p // bands, :, band_of(p)]

        for offset in far_first:
            p = peer(offset)
            remote(block(p), target.at[comp, rows_of(me)], send_sem.at[slot], recv_sem.at[slot], {"gx": p})
        pltpu.make_async_copy(block(me), target.at[comp, rows_of(me)], recv_sem.at[slot]).start()

    def to_blocks(source, target, base, comp, slot):
        place = target.at[comp, base + me // bands, :, band_of(me)]

        for offset in far_first:
            p = peer(offset)
            remote(source.at[comp, rows_of(p)], place, send_sem.at[slot], recv_sem.at[slot], {"gx": p})
        pltpu.make_async_copy(source.at[comp, rows_of(me)], place, recv_sem.at[slot]).start()

    def send_halo(fields, slot):
        @pl.when(gz > 0)
        def _():
            remote(fields.at[:, 1], fields.at[:, levels + 1], halo_send.at[slot, 0], halo_recv.at[slot, 0], {"gz": gz - 1})

        @pl.when(gz < sheets - 1)
        def _():
            remote(fields.at[:, levels], fields.at[:, 0], halo_send.at[slot, 1], halo_recv.at[slot, 1], {"gz": gz + 1})

    def wait_halo(fields, slot):
        @pl.when(gz > 0)
        def _():
            wait(fields.at[:, 0], halo_recv.at[slot, 1])

        @pl.when(gz < sheets - 1)
        def _():
            wait(fields.at[:, levels + 1], halo_recv.at[slot, 0])

    def wait_halo_sent(fields, slot):
        @pl.when(gz > 0)
        def _():
            wait(fields.at[:, 1], halo_send.at[slot, 0])

        @pl.when(gz < sheets - 1)
        def _():
            wait(fields.at[:, levels], halo_send.at[slot, 1])

    loads = [pltpu.make_async_copy(v_hbm.at[c], v_raw.at[c], load_sem.at[c]) for c in range(3)]
    loads += [
        pltpu.make_async_copy(inverse_hbm, inverse, load_sem.at[3]),
        pltpu.make_async_copy(forward_hbm, forward, load_sem.at[4]),
        pltpu.make_async_copy(drag_hbm, drag_raw, load_sem.at[5]),
        pltpu.make_async_copy(lam_hbm, lam, load_sem.at[6]),
    ]
    for load in loads:
        load.start()
    barrier = pltpu.get_barrier_semaphore()

    def greet(k, carry):
        pl.semaphore_signal(barrier, inc=1, device_id={"gx": (me + k) % groups}, device_id_type=MESH)
        return carry

    lax.fori_loop(1, groups, greet, 0)
    pl.semaphore_signal(barrier, inc=1, device_id={"sec": 1 - sec}, device_id_type=MESH)

    @pl.when(gz > 0)
    def _():
        pl.semaphore_signal(barrier, inc=1, device_id={"gz": gz - 1}, device_id_type=MESH)

    @pl.when(gz < sheets - 1)
    def _():
        pl.semaphore_signal(barrier, inc=1, device_id={"gz": gz + 1}, device_id_type=MESH)

    for c in range(3):
        loads[c].wait()
        for z in range(levels):
            v_here[c, 1 + z] = v_raw[c, :, z, :]

    @pl.when((gz == 0) | (gz == sheets - 1))
    def _():
        pl.semaphore_wait(barrier, groups + 1)

    @pl.when((gz > 0) & (gz < sheets - 1))
    def _():
        pl.semaphore_wait(barrier, groups + 2)

    send_halo(v_here, 0)
    for c in range(3):
        to_pencils(v_here, 1, v_pen, c, c)

    @pl.when(gz == 0)
    def _():
        v_here[:, 0] = jnp.zeros((3, cells, width), F32)
        f_here[:, 0] = jnp.zeros((3, cells, width), F32)

    @pl.when(gz == sheets - 1)
    def _():
        v_here[:, levels + 1] = jnp.zeros((3, cells, width), F32)
        f_here[:, levels + 1] = jnp.zeros((3, cells, width), F32)

    loads[3].wait()
    loads[4].wait()

    def build(j, carry):
        kind = j // 2
        scaled_high, scaled_low = split(inverse[kind] * weights[pl.ds(j, 1), :])
        matrix = dot(scaled_high, forward[kind, 0]) + (
            dot(scaled_low, forward[kind, 0]) + dot(scaled_high, forward[kind, 1])
        )
        table[j, 0], table[j, 1] = split(matrix)
        return carry

    lax.fori_loop(0, 3, build, 0)
    loads[5].wait()
    for z in range(levels):
        drag[z] = drag_raw[:, z, :]

    def local_terms(fields, comp, put):
        def spread(z, carry):
            at = pl.ds(pl.multiple_of(z * cells, cells), cells)
            low_at = pl.ds(pl.multiple_of((levels + z) * cells, cells), cells)
            stack[at], stack[low_at] = split(fields[comp, 1 + z])
            return carry

        lax.fori_loop(0, levels, spread, 0)
        rows = levels * cells
        both = dot(stack[...], table[0, 0])
        span_grad[...] = (both[:rows] + both[rows:]) + dot(stack[:rows], table[0, 1])

        def level(z, carry):
            at = pl.ds(pl.multiple_of(z * cells, cells), cells)
            rise = 0.5 * (fields[comp, 2 + z] - fields[comp, z])
            here = fields[comp, 1 + z]
            advect = fields[1, 1 + z] * span_grad[at] + fields[2, 1 + z] * rise
            put(z, here, -advect - drag[z] * jnp.abs(fields[0, 1 + z]) * here)
            return carry

        lax.fori_loop(0, levels, level, 0)

    def stream_grad(fields, comp):
        near, far = fields[comp, :half], fields[comp, half:]
        parts = []
        for j, mixed in ((1, near + far), (2, near - far)):
            high, low = split(mixed)
            both = dot(table[j, 0], jnp.concatenate([high, low], 1))
            parts.append((both[:, :LANES] + both[:, LANES:]) + dot(table[j, 1], high))
        return parts[0] + parts[1], parts[0] - parts[1]

    wait_halo(v_here, 0)
    for c in range(3):

        def keep(z, here, value, c=c):
            h_here[c, z] = value

        local_terms(v_here, c, keep)
        wait(v_pen.at[c], recv_sem.at[c])

        @pl.when(sec == 0)
        def _(c=c):
            remote(v_pen.at[c, lift], up_v.at[c], up_send.at[c], up_recv.at[c], {"sec": 1})

        to_pencils(h_here, 0, h_pen, c, 3 + c)

    loads[6].wait()
    for c in range(3):
        near, far = stream_grad(v_pen, c)
        rest[c, :half] = v_pen[c, :half] - dt * (v_pen[0, :half] * near)
        rest[c, half:] = v_pen[c, half:] - dt * (v_pen[0, half:] * far)

    @pl.when(sec == 1)
    def _():
        for c in range(3):
            wait(up_v.at[c], up_recv.at[c])
            rest[c, lift] += dt * (lam[...] * (up_v[c] - v_pen[c, lift]))

    for c in range(3):
        wait(h_pen.at[c], recv_sem.at[3 + c])
        f_pen[c] = rest[c] + dt * h_pen[c]

        @pl.when(sec == 0)
        def _(c=c):
            remote(f_pen.at[c, lift], up_f.at[c], up_send.at[3 + c], up_recv.at[3 + c], {"sec": 1})

        to_blocks(f_pen, f_here, 1, c, 6 + c)

    for c in range(3):
        near, far = stream_grad(f_pen, c)
        g_pen[c, :half] = -f_pen[0, :half] * near
        g_pen[c, half:] = -f_pen[0, half:] * far

        @pl.when(sec == 1)
        def _(c=c):
            wait(up_f.at[c], up_recv.at[3 + c])
            g_pen[c, lift] += lam[...] * (up_f[c] - f_pen[c, lift])

        to_blocks(g_pen, g_here, 0, c, 9 + c)

    for c in range(3):
        wait(g_here.at[c], recv_sem.at[6 + c])
    send_halo(f_here, 1)
    wait_halo(f_here, 1)
    for c in range(3):

        def keep(z, here, value, c=c):
            partial[c, z] = 0.5 * v_here[c, 1 + z] + 0.5 * (here + dt * value)

        local_terms(f_here, c, keep)

    stores = []
    for c in range(3):
        wait(g_here.at[c], recv_sem.at[9 + c])
        for z in range(levels):
            out_raw[c, :, z, :] = partial[c, z] + (0.5 * dt) * g_here[c, z]
        store = pltpu.make_async_copy(out_raw.at[c], out_hbm.at[c], own_sem.at[c])
        store.start()
        stores.append(store)

    others = pl.ds(0, total - cells)
    for slot in range(12):
        wait(v_pen.at[0, others], send_sem.at[slot])
    wait_halo_sent(v_here, 0)
    wait_halo_sent(f_here, 1)

    @pl.when(sec == 0)
    def _():
        for c in range(3):
            wait(up_v.at[c], up_send.at[c])
            wait(up_f.at[c], up_send.at[3 + c])

    for store in stores:
        store.wait()


def solution(mesh):
    groups, sheets = mesh.shape["gx"], mesh.shape["gz"]

    def shards(velocity, drag, stream_gain, span_gain):
        fields, drag_here = velocity[0], drag[0]
        _, cells, levels, width = fields.shape
        total = cells * groups
        half = total // 2
        pencil = (3, total, LANES)
        block = (3, levels, cells, width)
        padded = (3, levels + 2, cells, width)
        fringe = total // 4
        forward, inverse = transform_tables(half)
        high, low = halves(forward)
        forward = np.stack([high, low], 1)
        phases = np.pi * (np.arange(fringe) + 0.5) / fringe
        lam = np.repeat((fringe_peak * np.sin(phases) ** 2)[:, None], LANES, 1)
        weights = mode_weights(stream_gain, span_gain, total, width)
        dma = pltpu.SemaphoreType.DMA
        flops = 2 * 3 * (2 * total * half * LANES * 4 + 2 * half * half * half * 3)
        out = pl.pallas_call(
            functools.partial(step_kernel, groups, sheets),
            name="fringe_step",
            out_shape=jax.ShapeDtypeStruct(fields.shape, F32),
            in_specs=[pl.BlockSpec(memory_space=ANY)] * 2
            + [pl.BlockSpec(memory_space=pltpu.VMEM)]
            + [pl.BlockSpec(memory_space=ANY)] * 3,
            out_specs=pl.BlockSpec(memory_space=ANY),
            scratch_shapes=[
                pltpu.VMEM(fields.shape, F32),
                pltpu.VMEM(drag_here.shape, F32),
                pltpu.VMEM(fields.shape, F32),
                pltpu.VMEM((2, 2, half, half), BF16),
                pltpu.VMEM((2, half, half), F32),
                pltpu.VMEM((fringe, LANES), F32),
                pltpu.VMEM((3, 2, half, half), BF16),
                pltpu.VMEM(padded, F32),
                pltpu.VMEM(padded, F32),
                pltpu.VMEM((levels, cells, width), F32),
                pltpu.VMEM(block, F32),
                pltpu.VMEM(block, F32),
                pltpu.VMEM(block, F32),
                pltpu.VMEM((2 * levels * cells, width), BF16),
                pltpu.VMEM((levels * cells, width), F32),
                pltpu.VMEM(pencil, F32),
                pltpu.VMEM(pencil, F32),
                pltpu.VMEM(pencil, F32),
                pltpu.VMEM(pencil, F32),
                pltpu.VMEM(pencil, F32),
                pltpu.VMEM((3, fringe, LANES), F32),
                pltpu.VMEM((3, fringe, LANES), F32),
                dma((7,)),
                dma((3,)),
                dma((12,)),
                dma((12,)),
                dma((2, 2)),
                dma((2, 2)),
                dma((6,)),
                dma((6,)),
            ],
            compiler_params=pltpu.CompilerParams(
                collective_id=0, has_side_effects=True, vmem_limit_bytes=56 * 2**20
            ),
            cost_estimate=pl.CostEstimate(flops=flops, bytes_accessed=10**7, transcendentals=0),
        )(fields, drag_here, weights, forward, inverse.astype(np.float32), lam.astype(np.float32))
        return out[None]

    return jax.shard_map(
        shards,
        mesh=mesh,
        in_specs=(P("sec", None, "gx", "gz", None), P("sec", "gx", "gz", None), P(), P()),
        out_specs=P("sec", None, "gx", "gz", None),
        check_vma=False,
    )
```

```python
import functools

import jax
import jax.numpy as jnp
import ml_dtypes
import numpy as np
from jax import lax
from jax.experimental import pallas as pl
from jax.experimental.pallas import tpu as pltpu
from jax.sharding import PartitionSpec as P

MESH = pl.DeviceIdType.MESH
ANY = pl.ANY
F32 = jnp.float32
BF16 = jnp.bfloat16
fringe_peak = 4.0
dt = 0.05
LANES = 128


def halves(x):
    high = x.astype(np.float32).astype(ml_dtypes.bfloat16)
    low = (x - high.astype(np.float64)).astype(ml_dtypes.bfloat16)
    return high, low


def transform_tables(half):
    points = np.arange(half, dtype=np.int64)
    forward, inverse = [], []
    for odd in range(2):
        modes = 2 * np.arange(half // 2, dtype=np.int64) + odd
        angle = 2.0 * np.pi * (np.outer(modes, points) % (2 * half)) / (2 * half)
        forward.append(np.concatenate([np.cos(angle), np.sin(angle)], 0))
        inverse.append(np.concatenate([-np.sin(angle), np.cos(angle)], 0).T)
    return np.stack(forward), np.stack(inverse)


def wave_numbers(total_x, width_y):
    rows = np.zeros((2, total_x // 2))
    rows[0, : width_y // 2] = -(2.0 / width_y) * 2.0 * np.pi / width_y * np.arange(width_y // 2)
    rows[1] = (2.0 / total_x) * 2.0 * np.pi / total_x * np.arange(total_x // 2)
    return rows.astype(np.float32)


def even_then_odd(half):
    order = np.concatenate([np.arange(0, half, 2), np.arange(1, half, 2)])
    return (np.arange(half)[:, None] == order[None]).astype(ml_dtypes.bfloat16)


def split(x):
    high = x.astype(BF16)
    return high, (x - high.astype(F32)).astype(BF16)


def dot(a, b):
    return jnp.dot(a, b, preferred_element_type=F32)


def step_kernel(
    groups, sheets, v_hbm, drag_hbm, stream_hbm, span_hbm, wave_hbm, pick_hbm, forward_hbm, inverse_hbm, lam_hbm, out_raw,
    v_raw, drag_raw, stream_gain, span_gain, wave, pick, weights, forward, inverse, lam, table,
    v_here, f_here, drag, h_here, g_here, partial, stack, span_grad,
    v_pen, h_pen, f_pen, g_pen, rest, up_v, up_f,
    load_sem, send_sem, recv_sem, halo_send, halo_recv, up_send, up_recv, ready,
):
    me, gz, sec = lax.axis_index("gx"), lax.axis_index("gz"), lax.axis_index("sec")
    levels, cells, width = drag.shape
    half = table.shape[-1]
    total = 2 * half
    bands = width // LANES
    fringe = total - total // 4
    lift = pl.ds(fringe, total - fringe)
    shape_y, shape_x = 4, groups // 8

    far_first = sorted(
        [(y, x, core) for y in range(shape_y) for x in range(shape_x) for core in range(2)][1:],
        key=lambda o: -(min(o[0], shape_y - o[0]) + min(o[1], shape_x - o[1])),
    )

    def peer(offset):
        y = (me // (2 * shape_x) + offset[0]) % shape_y
        x = (me // 2 + offset[1]) % shape_x
        return (y * shape_x + x) * 2 + (me + offset[2]) % 2

    def rows_of(device):
        return pl.ds(pl.multiple_of(device * cells, cells), cells)

    def band_of(device):
        return pl.ds(pl.multiple_of((device % bands) * LANES, LANES), LANES)

    def wait(ref, sem):
        pltpu.make_async_copy(ref, ref, sem).wait()

    def remote(source, target, sent, arrived, where):
        pltpu.make_async_remote_copy(
            source, target, sent, arrived, device_id=where, device_id_type=MESH
        ).start()

    def to_pencils(source, base, target, comp, slot):
        def block(p):
            return source.at[comp, base + p // bands, :, band_of(p)]

        for offset in far_first:
            p = peer(offset)
            remote(block(p), target.at[comp, rows_of(me)], send_sem.at[slot], recv_sem.at[slot], {"gx": p})
        pltpu.make_async_copy(block(me), target.at[comp, rows_of(me)], recv_sem.at[slot]).start()

    def to_blocks(source, target, base, comp, slot):
        place = target.at[comp, base + me // bands, :, band_of(me)]

        for offset in far_first:
            p = peer(offset)
            remote(source.at[comp, rows_of(p)], place, send_sem.at[slot], recv_sem.at[slot], {"gx": p})
        pltpu.make_async_copy(source.at[comp, rows_of(me)], place, recv_sem.at[slot]).start()

    def send_halo(fields, slot):
        @pl.when(gz > 0)
        def _():
            remote(fields.at[:, 1], fields.at[:, levels + 1], halo_send.at[slot, 0], halo_recv.at[slot, 0], {"gz": gz - 1})

        @pl.when(gz < sheets - 1)
        def _():
            remote(fields.at[:, levels], fields.at[:, 0], halo_send.at[slot, 1], halo_recv.at[slot, 1], {"gz": gz + 1})

    def wait_halo(fields, slot):
        @pl.when(gz > 0)
        def _():
            wait(fields.at[:, 0], halo_recv.at[slot, 1])

        @pl.when(gz < sheets - 1)
        def _():
            wait(fields.at[:, levels + 1], halo_recv.at[slot, 0])

    def wait_halo_sent(fields, slot):
        @pl.when(gz > 0)
        def _():
            wait(fields.at[:, 1], halo_send.at[slot, 0])

        @pl.when(gz < sheets - 1)
        def _():
            wait(fields.at[:, levels], halo_send.at[slot, 1])

    loads = [pltpu.make_async_copy(v_hbm.at[c], v_raw.at[c], load_sem.at[c]) for c in range(3)]
    loads += [
        pltpu.make_async_copy(inverse_hbm, inverse, load_sem.at[3]),
        pltpu.make_async_copy(forward_hbm, forward, load_sem.at[4]),
        pltpu.make_async_copy(drag_hbm, drag_raw, load_sem.at[5]),
        pltpu.make_async_copy(lam_hbm, lam, load_sem.at[6]),
        pltpu.make_async_copy(stream_hbm, stream_gain, load_sem.at[7]),
        pltpu.make_async_copy(span_hbm, span_gain, load_sem.at[8]),
        pltpu.make_async_copy(wave_hbm, wave, load_sem.at[9]),
        pltpu.make_async_copy(pick_hbm, pick, load_sem.at[10]),
    ]
    for load in loads:
        load.start()
    barrier = pltpu.get_barrier_semaphore()

    def greet(k, carry):
        pl.semaphore_signal(barrier, inc=1, device_id={"gx": (me + k) % groups}, device_id_type=MESH)
        return carry

    lax.fori_loop(1, groups, greet, 0)
    @pl.when(sec == 0)
    def _():
        pl.semaphore_signal(barrier, inc=1, device_id={"sec": 1}, device_id_type=MESH)

    @pl.when(gz < sheets - 1)
    def _():
        pl.semaphore_signal(barrier, inc=1, device_id={"gz": gz + 1}, device_id_type=MESH)

    for c in range(3):
        loads[c].wait()
        for z in range(levels):
            v_here[c, 1 + z] = v_raw[c, :, z, :]
        if c == 0:
            pl.semaphore_wait(barrier, groups - 1 + jnp.minimum(gz, 1) + sec)
        to_pencils(v_here, 1, v_pen, c, c)
        if c == 0:

            @pl.when(gz > 0)
            def _():
                pl.semaphore_signal(ready.at[0], inc=1, device_id={"gz": gz - 1}, device_id_type=MESH)

            @pl.when(sec == 1)
            def _():
                pl.semaphore_signal(ready.at[1], inc=1, device_id={"sec": 0}, device_id_type=MESH)

    @pl.when(gz < sheets - 1)
    def _():
        pl.semaphore_wait(ready.at[0], 1)

    send_halo(v_here, 0)

    @pl.when(gz == 0)
    def _():
        v_here[:, 0] = jnp.zeros((3, cells, width), F32)
        f_here[:, 0] = jnp.zeros((3, cells, width), F32)

    @pl.when(gz == sheets - 1)
    def _():
        v_here[:, levels + 1] = jnp.zeros((3, cells, width), F32)
        f_here[:, levels + 1] = jnp.zeros((3, cells, width), F32)

    for load in loads[7:]:
        load.wait()
    quarter = half // 2
    along_y = span_gain[pl.ds(0, quarter)].reshape(1, quarter) * wave[0:1, :quarter]
    along_x = stream_gain[pl.ds(0, half)].reshape(1, half) * wave[1:2]
    sorted_x, left = jnp.zeros((16, half), F32), jnp.broadcast_to(along_x, (16, half))
    for _ in range(3):
        part = left.astype(BF16)
        sorted_x = sorted_x + dot(part, pick[...])
        left = left - part.astype(F32)
    weights[0:1, :] = jnp.concatenate([along_y, along_y], 1)
    weights[1:2, :] = jnp.concatenate([sorted_x[0:1, :quarter]] * 2, 1)
    weights[2:3, :] = jnp.concatenate([sorted_x[0:1, quarter:]] * 2, 1)
    loads[3].wait()
    loads[4].wait()

    def build(j, carry):
        kind = j // 2
        scaled_high, scaled_low = split(inverse[kind] * weights[pl.ds(j, 1), :])
        matrix = dot(scaled_high, forward[kind, 0]) + (
            dot(scaled_low, forward[kind, 0]) + dot(scaled_high, forward[kind, 1])
        )
        table[j, 0], table[j, 1] = split(matrix)
        return carry

    lax.fori_loop(0, 3, build, 0)
    loads[5].wait()
    for z in range(levels):
        drag[z] = drag_raw[:, z, :]

    def local_terms(fields, comp, put):
        def spread(z, carry):
            at = pl.ds(pl.multiple_of(z * cells, cells), cells)
            low_at = pl.ds(pl.multiple_of((levels + z) * cells, cells), cells)
            stack[at], stack[low_at] = split(fields[comp, 1 + z])
            return carry

        lax.fori_loop(0, levels, spread, 0)
        rows = levels * cells
        both = dot(stack[...], table[0, 0])
        span_grad[...] = (both[:rows] + both[rows:]) + dot(stack[:rows], table[0, 1])

        def level(z, carry):
            at = pl.ds(pl.multiple_of(z * cells, cells), cells)
            rise = 0.5 * (fields[comp, 2 + z] - fields[comp, z])
            here = fields[comp, 1 + z]
            advect = fields[1, 1 + z] * span_grad[at] + fields[2, 1 + z] * rise
            put(z, here, -advect - drag[z] * jnp.abs(fields[0, 1 + z]) * here)
            return carry

        lax.fori_loop(0, levels, level, 0)

    def stream_grad(fields, comp):
        near, far = fields[comp, :half], fields[comp, half:]
        parts = []
        for j, mixed in ((1, near + far), (2, near - far)):
            high, low = split(mixed)
            both = dot(table[j, 0], jnp.concatenate([high, low], 1))
            parts.append((both[:, :LANES] + both[:, LANES:]) + dot(table[j, 1], high))
        return parts[0] + parts[1], parts[0] - parts[1]

    wait_halo(v_here, 0)
    for c in range(3):

        def keep(z, here, value, c=c):
            h_here[c, z] = value

        local_terms(v_here, c, keep)
        wait(v_pen.at[c], recv_sem.at[c])

        @pl.when(sec == 0)
        def _(c=c):
            if c == 0:
                pl.semaphore_wait(ready.at[1], 1)
            remote(v_pen.at[c, lift], up_v.at[c], up_send.at[c], up_recv.at[c], {"sec": 1})

        to_pencils(h_here, 0, h_pen, c, 3 + c)

    loads[6].wait()
    for c in range(3):
        near, far = stream_grad(v_pen, c)
        rest[c, :half] = v_pen[c, :half] - dt * (v_pen[0, :half] * near)
        rest[c, half:] = v_pen[c, half:] - dt * (v_pen[0, half:] * far)

    @pl.when(sec == 1)
    def _():
        for c in range(3):
            wait(up_v.at[c], up_recv.at[c])
            rest[c, lift] += dt * (lam[...] * (up_v[c] - v_pen[c, lift]))

    for c in range(3):
        wait(h_pen.at[c], recv_sem.at[3 + c])
        f_pen[c] = rest[c] + dt * h_pen[c]

        @pl.when(sec == 0)
        def _(c=c):
            remote(f_pen.at[c, lift], up_f.at[c], up_send.at[3 + c], up_recv.at[3 + c], {"sec": 1})

        to_blocks(f_pen, f_here, 1, c, 6 + c)

    for c in range(3):
        near, far = stream_grad(f_pen, c)
        g_pen[c, :half] = -f_pen[0, :half] * near
        g_pen[c, half:] = -f_pen[0, half:] * far

        @pl.when(sec == 1)
        def _(c=c):
            wait(up_f.at[c], up_recv.at[3 + c])
            g_pen[c, lift] += lam[...] * (up_f[c] - f_pen[c, lift])

        to_blocks(g_pen, g_here, 0, c, 9 + c)

    for c in range(3):
        wait(g_here.at[c], recv_sem.at[6 + c])
    send_halo(f_here, 1)
    wait_halo(f_here, 1)
    for c in range(3):

        def keep(z, here, value, c=c):
            partial[c, z] = 0.5 * v_here[c, 1 + z] + 0.5 * (here + dt * value)

        local_terms(f_here, c, keep)

    for c in range(3):
        wait(g_here.at[c], recv_sem.at[9 + c])
        for z in range(levels):
            out_raw[c, :, z, :] = partial[c, z] + (0.5 * dt) * g_here[c, z]

    others = pl.ds(0, total - cells)
    for slot in range(12):
        wait(v_pen.at[0, others], send_sem.at[slot])
    wait_halo_sent(v_here, 0)
    wait_halo_sent(f_here, 1)

    @pl.when(sec == 0)
    def _():
        for c in range(3):
            wait(up_v.at[c], up_send.at[c])
            wait(up_f.at[c], up_send.at[3 + c])


def solution(mesh):
    groups, sheets = mesh.shape["gx"], mesh.shape["gz"]

    def shards(velocity, drag, stream_gain, span_gain):
        fields, drag_here = velocity[0], drag[0]
        _, cells, levels, width = fields.shape
        total = cells * groups
        half = total // 2
        pencil = (3, total, LANES)
        block = (3, levels, cells, width)
        padded = (3, levels + 2, cells, width)
        fringe = total // 4
        forward, inverse = transform_tables(half)
        high, low = halves(forward)
        forward = np.stack([high, low], 1)
        phases = np.pi * (np.arange(fringe) + 0.5) / fringe
        lam = np.repeat((fringe_peak * np.sin(phases) ** 2)[:, None], LANES, 1)
        wave, pick = wave_numbers(total, width), even_then_odd(half)
        dma = pltpu.SemaphoreType.DMA
        flops = 2 * 3 * (2 * total * half * LANES * 4 + 2 * half * half * half * 3)
        out = pl.pallas_call(
            functools.partial(step_kernel, groups, sheets),
            name="fringe_step",
            out_shape=pltpu.VMEM(fields.shape, F32),
            in_specs=[pl.BlockSpec(memory_space=ANY)] * 9,
            out_specs=pl.BlockSpec(memory_space=pltpu.VMEM),
            scratch_shapes=[
                pltpu.VMEM(fields.shape, F32),
                pltpu.VMEM(drag_here.shape, F32),
                pltpu.VMEM(stream_gain.shape, F32),
                pltpu.VMEM(span_gain.shape, F32),
                pltpu.VMEM((2, half), F32),
                pltpu.VMEM((half, half), BF16),
                pltpu.VMEM((8, half), F32),
                pltpu.VMEM((2, 2, half, half), BF16),
                pltpu.VMEM((2, half, half), F32),
                pltpu.VMEM((fringe, LANES), F32),
                pltpu.VMEM((3, 2, half, half), BF16),
                pltpu.VMEM(padded, F32),
                pltpu.VMEM(padded, F32),
                pltpu.VMEM((levels, cells, width), F32),
                pltpu.VMEM(block, F32),
                pltpu.VMEM(block, F32),
                pltpu.VMEM(block, F32),
                pltpu.VMEM((2 * levels * cells, width), BF16),
                pltpu.VMEM((levels * cells, width), F32),
                pltpu.VMEM(pencil, F32),
                pltpu.VMEM(pencil, F32),
                pltpu.VMEM(pencil, F32),
                pltpu.VMEM(pencil, F32),
                pltpu.VMEM(pencil, F32),
                pltpu.VMEM((3, fringe, LANES), F32),
                pltpu.VMEM((3, fringe, LANES), F32),
                dma((11,)),
                dma((12,)),
                dma((12,)),
                dma((2, 2)),
                dma((2, 2)),
                dma((6,)),
                dma((6,)),
                pltpu.SemaphoreType.REGULAR((2,)),
            ],
            compiler_params=pltpu.CompilerParams(
                collective_id=0, has_side_effects=True, vmem_limit_bytes=56 * 2**20
            ),
            cost_estimate=pl.CostEstimate(flops=flops, bytes_accessed=10**7, transcendentals=0),
        )(
            fields, drag_here, stream_gain, span_gain, wave, pick,
            forward, inverse.astype(np.float32), lam.astype(np.float32),
        )
        return out[None]

    return jax.shard_map(
        shards,
        mesh=mesh,
        in_specs=(P("sec", None, "gx", "gz", None), P("sec", "gx", "gz", None), P(), P()),
        out_specs=P("sec", None, "gx", "gz", None),
        check_vma=False,
    )
```

```python
import functools

import jax
import jax.numpy as jnp
import ml_dtypes
import numpy as np
from jax import lax
from jax.experimental import pallas as pl
from jax.experimental.pallas import tpu as pltpu
from jax.sharding import PartitionSpec as P

MESH = pl.DeviceIdType.MESH
ANY = pl.ANY
F32 = jnp.float32
BF16 = jnp.bfloat16
fringe_peak = 4.0
dt = 0.05
LANES = 128


def halves(x):
    high = x.astype(np.float32).astype(ml_dtypes.bfloat16)
    low = (x - high.astype(np.float64)).astype(ml_dtypes.bfloat16)
    return high, low


def transform_tables(half):
    points = np.arange(half, dtype=np.int64)
    forward, inverse = [], []
    for odd in range(2):
        modes = 2 * np.arange(half // 2, dtype=np.int64) + odd
        angle = 2.0 * np.pi * (np.outer(modes, points) % (2 * half)) / (2 * half)
        forward.append(np.concatenate([np.cos(angle), np.sin(angle)], 0))
        inverse.append(np.concatenate([-np.sin(angle), np.cos(angle)], 0).T)
    return np.stack(forward), np.stack(inverse)


def wave_numbers(total_x, width_y):
    rows = np.zeros((2, total_x // 2))
    rows[0, : width_y // 2] = -(2.0 / width_y) * 2.0 * np.pi / width_y * np.arange(width_y // 2)
    rows[1] = (2.0 / total_x) * 2.0 * np.pi / total_x * np.arange(total_x // 2)
    return rows.astype(np.float32)


def even_then_odd(half):
    order = np.concatenate([np.arange(0, half, 2), np.arange(1, half, 2)])
    return (np.arange(half)[:, None] == order[None]).astype(ml_dtypes.bfloat16)


def split(x):
    high = x.astype(BF16)
    return high, (x - high.astype(F32)).astype(BF16)


def dot(a, b):
    return jnp.dot(a, b, preferred_element_type=F32)


def step_kernel(
    groups, sheets, v_hbm, drag_hbm, stream_hbm, span_hbm, wave_hbm, pick_hbm, forward_hbm, inverse_hbm, lam_hbm, out_raw,
    v_raw, drag_raw, stream_gain, span_gain, wave, pick, weights, forward, inverse, lam, table,
    v_here, f_here, drag, h_here, g_here, partial, stack, span_grad,
    v_pen, h_pen, f_pen, g_pen, rest, up_v, up_f,
    load_sem, send_sem, recv_sem, halo_send, halo_recv, up_send, up_recv, ready,
):
    me, gz, sec = lax.axis_index("gx"), lax.axis_index("gz"), lax.axis_index("sec")
    levels, cells, width = drag.shape
    half = table.shape[-1]
    total = 2 * half
    bands = width // LANES
    fringe = total - total // 4
    lift = pl.ds(fringe, total - fringe)
    shape_y, shape_x = 4, groups // 8

    far_first = sorted(
        [(y, x, core) for y in range(shape_y) for x in range(shape_x) for core in range(2)][1:],
        key=lambda o: -(min(o[0], shape_y - o[0]) + min(o[1], shape_x - o[1])),
    )

    def peer(offset):
        y = (me // (2 * shape_x) + offset[0]) % shape_y
        x = (me // 2 + offset[1]) % shape_x
        return (y * shape_x + x) * 2 + (me + offset[2]) % 2

    def rows_of(device):
        return pl.ds(pl.multiple_of(device * cells, cells), cells)

    def band_of(device):
        return pl.ds(pl.multiple_of((device % bands) * LANES, LANES), LANES)

    def wait(ref, sem):
        pltpu.make_async_copy(ref, ref, sem).wait()

    def remote(source, target, sent, arrived, where):
        pltpu.make_async_remote_copy(
            source, target, sent, arrived, device_id=where, device_id_type=MESH
        ).start()

    def to_pencils(source, base, target, comp, slot):
        def block(p):
            return source.at[comp, base + p // bands, :, band_of(p)]

        for offset in far_first:
            p = peer(offset)
            remote(block(p), target.at[comp, rows_of(me)], send_sem.at[slot], recv_sem.at[slot], {"gx": p})
        pltpu.make_async_copy(block(me), target.at[comp, rows_of(me)], recv_sem.at[slot]).start()

    def to_blocks(source, target, base, comp, slot):
        place = target.at[comp, base + me // bands, :, band_of(me)]

        for offset in far_first:
            p = peer(offset)
            remote(source.at[comp, rows_of(p)], place, send_sem.at[slot], recv_sem.at[slot], {"gx": p})
        pltpu.make_async_copy(source.at[comp, rows_of(me)], place, recv_sem.at[slot]).start()

    def send_halo(fields, slot):
        @pl.when(gz > 0)
        def _():
            remote(fields.at[:, 1], fields.at[:, levels + 1], halo_send.at[slot, 0], halo_recv.at[slot, 0], {"gz": gz - 1})

        @pl.when(gz < sheets - 1)
        def _():
            remote(fields.at[:, levels], fields.at[:, 0], halo_send.at[slot, 1], halo_recv.at[slot, 1], {"gz": gz + 1})

    def wait_halo(fields, slot):
        @pl.when(gz > 0)
        def _():
            wait(fields.at[:, 0], halo_recv.at[slot, 1])

        @pl.when(gz < sheets - 1)
        def _():
            wait(fields.at[:, levels + 1], halo_recv.at[slot, 0])

    def wait_halo_sent(fields, slot):
        @pl.when(gz > 0)
        def _():
            wait(fields.at[:, 1], halo_send.at[slot, 0])

        @pl.when(gz < sheets - 1)
        def _():
            wait(fields.at[:, levels], halo_send.at[slot, 1])

    loads = [pltpu.make_async_copy(v_hbm.at[c], v_raw.at[c], load_sem.at[c]) for c in range(3)]
    loads += [
        pltpu.make_async_copy(inverse_hbm, inverse, load_sem.at[3]),
        pltpu.make_async_copy(forward_hbm, forward, load_sem.at[4]),
        pltpu.make_async_copy(drag_hbm, drag_raw, load_sem.at[5]),
        pltpu.make_async_copy(lam_hbm, lam, load_sem.at[6]),
        pltpu.make_async_copy(stream_hbm, stream_gain, load_sem.at[7]),
        pltpu.make_async_copy(span_hbm, span_gain, load_sem.at[8]),
        pltpu.make_async_copy(wave_hbm, wave, load_sem.at[9]),
        pltpu.make_async_copy(pick_hbm, pick, load_sem.at[10]),
    ]
    loads[0].start()
    barrier = pltpu.get_barrier_semaphore()

    def greet(k, carry):
        pl.semaphore_signal(barrier, inc=1, device_id={"gx": (me + k) % groups}, device_id_type=MESH)
        return carry

    lax.fori_loop(1, groups, greet, 0)
    @pl.when(sec == 0)
    def _():
        pl.semaphore_signal(barrier, inc=1, device_id={"sec": 1}, device_id_type=MESH)

    @pl.when(gz < sheets - 1)
    def _():
        pl.semaphore_signal(barrier, inc=1, device_id={"gz": gz + 1}, device_id_type=MESH)

    loads[1].start()
    loads[2].start()
    for c in range(3):
        loads[c].wait()
        for z in range(levels):
            v_here[c, 1 + z] = v_raw[c, :, z, :]
        if c == 0:
            pl.semaphore_wait(barrier, groups - 1 + jnp.minimum(gz, 1) + sec)
        to_pencils(v_here, 1, v_pen, c, c)
        if c == 0:
            for load in loads[3:]:
                load.start()

            @pl.when(gz > 0)
            def _():
                pl.semaphore_signal(ready.at[0], inc=1, device_id={"gz": gz - 1}, device_id_type=MESH)

            @pl.when(sec == 1)
            def _():
                pl.semaphore_signal(ready.at[1], inc=1, device_id={"sec": 0}, device_id_type=MESH)

    @pl.when(gz < sheets - 1)
    def _():
        pl.semaphore_wait(ready.at[0], 1)

    send_halo(v_here, 0)

    @pl.when(gz == 0)
    def _():
        v_here[:, 0] = jnp.zeros((3, cells, width), F32)
        f_here[:, 0] = jnp.zeros((3, cells, width), F32)

    @pl.when(gz == sheets - 1)
    def _():
        v_here[:, levels + 1] = jnp.zeros((3, cells, width), F32)
        f_here[:, levels + 1] = jnp.zeros((3, cells, width), F32)

    for load in loads[7:]:
        load.wait()
    quarter = half // 2
    along_y = span_gain[pl.ds(0, quarter)].reshape(1, quarter) * wave[0:1, :quarter]
    along_x = stream_gain[pl.ds(0, half)].reshape(1, half) * wave[1:2]
    sorted_x, left = jnp.zeros((16, half), F32), jnp.broadcast_to(along_x, (16, half))
    for _ in range(3):
        part = left.astype(BF16)
        sorted_x = sorted_x + dot(part, pick[...])
        left = left - part.astype(F32)
    weights[0:1, :] = jnp.concatenate([along_y, along_y], 1)
    weights[1:2, :] = jnp.concatenate([sorted_x[0:1, :quarter]] * 2, 1)
    weights[2:3, :] = jnp.concatenate([sorted_x[0:1, quarter:]] * 2, 1)
    loads[3].wait()
    loads[4].wait()

    def build(j, carry):
        kind = j // 2
        scaled_high, scaled_low = split(inverse[kind] * weights[pl.ds(j, 1), :])
        matrix = dot(scaled_high, forward[kind, 0]) + (
            dot(scaled_low, forward[kind, 0]) + dot(scaled_high, forward[kind, 1])
        )
        table[j, 0], table[j, 1] = split(matrix)
        return carry

    lax.fori_loop(0, 3, build, 0)
    loads[5].wait()
    for z in range(levels):
        drag[z] = drag_raw[:, z, :]

    def local_terms(fields, comp, put):
        def spread(z, carry):
            at = pl.ds(pl.multiple_of(z * cells, cells), cells)
            low_at = pl.ds(pl.multiple_of((levels + z) * cells, cells), cells)
            stack[at], stack[low_at] = split(fields[comp, 1 + z])
            return carry

        lax.fori_loop(0, levels, spread, 0)
        rows = levels * cells
        both = dot(stack[...], table[0, 0])
        span_grad[...] = (both[:rows] + both[rows:]) + dot(stack[:rows], table[0, 1])

        def level(z, carry):
            at = pl.ds(pl.multiple_of(z * cells, cells), cells)
            rise = 0.5 * (fields[comp, 2 + z] - fields[comp, z])
            here = fields[comp, 1 + z]
            advect = fields[1, 1 + z] * span_grad[at] + fields[2, 1 + z] * rise
            put(z, here, -advect - drag[z] * jnp.abs(fields[0, 1 + z]) * here)
            return carry

        lax.fori_loop(0, levels, level, 0)

    def stream_grad(fields, comp):
        near, far = fields[comp, :half], fields[comp, half:]
        parts = []
        for j, mixed in ((1, near + far), (2, near - far)):
            high, low = split(mixed)
            both = dot(table[j, 0], jnp.concatenate([high, low], 1))
            parts.append((both[:, :LANES] + both[:, LANES:]) + dot(table[j, 1], high))
        return parts[0] + parts[1], parts[0] - parts[1]

    wait_halo(v_here, 0)
    for c in range(3):

        def keep(z, here, value, c=c):
            h_here[c, z] = value

        local_terms(v_here, c, keep)
        wait(v_pen.at[c], recv_sem.at[c])

        @pl.when(sec == 0)
        def _(c=c):
            if c == 0:
                pl.semaphore_wait(ready.at[1], 1)
            remote(v_pen.at[c, lift], up_v.at[c], up_send.at[c], up_recv.at[c], {"sec": 1})

        to_pencils(h_here, 0, h_pen, c, 3 + c)

    loads[6].wait()
    for c in range(3):
        near, far = stream_grad(v_pen, c)
        rest[c, :half] = v_pen[c, :half] - dt * (v_pen[0, :half] * near)
        rest[c, half:] = v_pen[c, half:] - dt * (v_pen[0, half:] * far)

    @pl.when(sec == 1)
    def _():
        for c in range(3):
            wait(up_v.at[c], up_recv.at[c])
            rest[c, lift] += dt * (lam[...] * (up_v[c] - v_pen[c, lift]))

    for c in range(3):
        wait(h_pen.at[c], recv_sem.at[3 + c])
        f_pen[c] = rest[c] + dt * h_pen[c]

        @pl.when(sec == 0)
        def _(c=c):
            remote(f_pen.at[c, lift], up_f.at[c], up_send.at[3 + c], up_recv.at[3 + c], {"sec": 1})

        to_blocks(f_pen, f_here, 1, c, 6 + c)

    for c in range(3):
        near, far = stream_grad(f_pen, c)
        g_pen[c, :half] = -f_pen[0, :half] * near
        g_pen[c, half:] = -f_pen[0, half:] * far

        @pl.when(sec == 1)
        def _(c=c):
            wait(up_f.at[c], up_recv.at[3 + c])
            g_pen[c, lift] += lam[...] * (up_f[c] - f_pen[c, lift])

        to_blocks(g_pen, g_here, 0, c, 9 + c)

    for c in range(3):
        wait(g_here.at[c], recv_sem.at[6 + c])
    send_halo(f_here, 1)
    wait_halo(f_here, 1)
    for c in range(3):

        def keep(z, here, value, c=c):
            partial[c, z] = 0.5 * v_here[c, 1 + z] + 0.5 * (here + dt * value)

        local_terms(f_here, c, keep)

    for c in range(3):
        wait(g_here.at[c], recv_sem.at[9 + c])
        for z in range(levels):
            out_raw[c, :, z, :] = partial[c, z] + (0.5 * dt) * g_here[c, z]

    others = pl.ds(0, total - cells)
    for slot in range(12):
        wait(v_pen.at[0, others], send_sem.at[slot])
    wait_halo_sent(v_here, 0)
    wait_halo_sent(f_here, 1)

    @pl.when(sec == 0)
    def _():
        for c in range(3):
            wait(up_v.at[c], up_send.at[c])
            wait(up_f.at[c], up_send.at[3 + c])


def solution(mesh):
    groups, sheets = mesh.shape["gx"], mesh.shape["gz"]

    def shards(velocity, drag, stream_gain, span_gain):
        fields, drag_here = velocity[0], drag[0]
        _, cells, levels, width = fields.shape
        total = cells * groups
        half = total // 2
        pencil = (3, total, LANES)
        block = (3, levels, cells, width)
        padded = (3, levels + 2, cells, width)
        fringe = total // 4
        forward, inverse = transform_tables(half)
        high, low = halves(forward)
        forward = np.stack([high, low], 1)
        phases = np.pi * (np.arange(fringe) + 0.5) / fringe
        lam = np.repeat((fringe_peak * np.sin(phases) ** 2)[:, None], LANES, 1)
        wave, pick = wave_numbers(total, width), even_then_odd(half)
        dma = pltpu.SemaphoreType.DMA
        flops = 2 * 3 * (2 * total * half * LANES * 4 + 2 * half * half * half * 3)
        out = pl.pallas_call(
            functools.partial(step_kernel, groups, sheets),
            name="fringe_step",
            out_shape=pltpu.VMEM(fields.shape, F32),
            in_specs=[pl.BlockSpec(memory_space=ANY)] * 9,
            out_specs=pl.BlockSpec(memory_space=pltpu.VMEM),
            scratch_shapes=[
                pltpu.VMEM(fields.shape, F32),
                pltpu.VMEM(drag_here.shape, F32),
                pltpu.VMEM(stream_gain.shape, F32),
                pltpu.VMEM(span_gain.shape, F32),
                pltpu.VMEM((2, half), F32),
                pltpu.VMEM((half, half), BF16),
                pltpu.VMEM((8, half), F32),
                pltpu.VMEM((2, 2, half, half), BF16),
                pltpu.VMEM((2, half, half), F32),
                pltpu.VMEM((fringe, LANES), F32),
                pltpu.VMEM((3, 2, half, half), BF16),
                pltpu.VMEM(padded, F32),
                pltpu.VMEM(padded, F32),
                pltpu.VMEM((levels, cells, width), F32),
                pltpu.VMEM(block, F32),
                pltpu.VMEM(block, F32),
                pltpu.VMEM(block, F32),
                pltpu.VMEM((2 * levels * cells, width), BF16),
                pltpu.VMEM((levels * cells, width), F32),
                pltpu.VMEM(pencil, F32),
                pltpu.VMEM(pencil, F32),
                pltpu.VMEM(pencil, F32),
                pltpu.VMEM(pencil, F32),
                pltpu.VMEM(pencil, F32),
                pltpu.VMEM((3, fringe, LANES), F32),
                pltpu.VMEM((3, fringe, LANES), F32),
                dma((11,)),
                dma((12,)),
                dma((12,)),
                dma((2, 2)),
                dma((2, 2)),
                dma((6,)),
                dma((6,)),
                pltpu.SemaphoreType.REGULAR((2,)),
            ],
            compiler_params=pltpu.CompilerParams(
                collective_id=0, has_side_effects=True, vmem_limit_bytes=56 * 2**20
            ),
            cost_estimate=pl.CostEstimate(flops=flops, bytes_accessed=10**7, transcendentals=0),
        )(
            fields, drag_here, stream_gain, span_gain, wave, pick,
            forward, inverse.astype(np.float32), lam.astype(np.float32),
        )
        return out[None]

    return jax.shard_map(
        shards,
        mesh=mesh,
        in_specs=(P("sec", None, "gx", "gz", None), P("sec", "gx", "gz", None), P(), P()),
        out_specs=P("sec", None, "gx", "gz", None),
        check_vma=False,
    )
```
